1024 devices in a mesh: dp: 64 (over x, z), tensor: 16 (over y, core).
Axes of the slice: x: 4, y: 8, z: 16, core: 2. Of those that a mesh axis runs over, the one named last changes fastest.
Arguments:
- residual: bfloat16 [65536, 4096], P(('dp', 'tensor')), may hold values from -6 to 6
- expert_hidden: bfloat16 [1024, 256, 768], P(('dp', 'tensor')), may hold values from -6 to 6
- down_weight: bfloat16 [16, 768, 4096], P('tensor'), may hold values from -0.21875 to 0.21875
- gates: float32 [65536, 2], P(('dp', 'tensor')), may hold values from 0.1 to 0.9
- routes: int32 [65536, 2], P(('dp', 'tensor')), may hold values from 0 to 15, all different within a row; in each aligned block of 64 rows (0 to 63, 64 to 127, ...) at most 16 rows name the same one
- router_probs: float32 [65536, 16], P(('dp', 'tensor')), may hold values from 0 to 14
- norm_gain: float32 [4096], replicated, may hold values from 0.5 to 1.5
- qkv_weight: bfloat16 [4096, 5120], P(None, 'tensor'), may hold values from -0.09375 to 0.09375
Outputs:
- new_residual: bfloat16 [65536, 4096], P(('dp', 'tensor'))
- qkv: bfloat16 [65536, 5120], P('dp', 'tensor')
- balance: float32 [], replicated
The draws below stay inside these ranges and needn't reach their ends.
Inputs may be any that keep to these rules, and one draw needn't show every extreme that they name: `routes`: within the rows of one device (aligned blocks of 64 tokens) a token names 2 different experts and no expert is named by more than 16 tokens; some expert is named by exactly 16 in some blocks.
All inputs are finite; a program needn't handle non-finite values.
Results may differ from the reference program's by a relative error of at most 0.006.
Values may be sent and summed in bfloat16 or wider, within the bound.
No kernel may reach another device: no remote copies, remote signals or barrier semaphores. Data moves between devices by JAX's collectives and lax.ppermute only.
A program may use at most 64 MiB of HBM per device.

```python
import math
import jax
import jax.numpy as jnp
import numpy as np
from jax import lax

D = 4096
FF = 768
TOP = 2
TOK_DEV = 64
EXPERTS = 16
GROUP = 1024
TOKENS = 65536
CAP = 16
QKVC = 5120
N_DP = 64
N_TENSOR = 16


def draw_router_probs(key, part):
    key = jax.random.fold_in(key, 11)
    first, second, third, fourth = jax.random.split(key, 4)
    position = jnp.arange(TOKENS, dtype=jnp.float32) / TOKENS
    block_count = TOKENS // TOK_DEV
    block_factor = jnp.exp(jax.random.uniform(fourth, (block_count, 1), jnp.float32, math.log(0.001), 0.0))
    block_factor = jnp.repeat(block_factor, TOK_DEV, axis=0)
    level = 0.03
    rising = jnp.exp(math.log(3.0) * position)[:, None]
    row_scale = jnp.exp(jax.random.uniform(first, (TOKENS, 1), jnp.float32, 0.0, math.log(10.0)))
    column_scale = jnp.exp(jax.random.uniform(second, (1, EXPERTS), jnp.float32, 0.0, math.log(10.0)))
    base = jax.random.uniform(third, (TOKENS, EXPERTS), jnp.float32, 0.5, 1.5)
    return (level * rising * row_scale * column_scale * base * block_factor).astype(jnp.float32)


def levels(own_key, extent, cuts, smallest, high):
    factor_of, own = 1.0, jax.random.fold_in(own_key, 6)
    for dim, parts in cuts:
        heights = jnp.exp(jax.random.uniform(jax.random.fold_in(own, dim), (parts,), jnp.float32, smallest / len(cuts), high / len(cuts)))
        factor_of = factor_of * jnp.repeat(heights, extent[dim] // parts).reshape([-1 if axis == dim else 1 for axis in range(len(extent))])
    return factor_of


def shared_out(stream_key, own, number, rows, count, top, reach, lean):
    order = jax.random.permutation(stream_key, count)
    crowded, common = load_shares(count, rows * top, reach, lean, True), load_shares(count, rows * top, reach, lean, False)
    places = jnp.arange(count)

    def named(lengths, turn):
        used = int((lengths > 0).sum())
        fixed = max(1, used // 4)
        passed = fixed + (places - fixed + turn * (used - fixed)) % max(1, count - fixed)
        return jnp.zeros((count,), jnp.int32).at[order[jnp.where(places < fixed, places, passed)]].set(jnp.asarray(lengths, jnp.int32))

    lengths = jnp.where(number % 4 == 0, named(crowded, number // 4), named(common, number - number // 4 - 1))
    mixed = jax.random.permutation(jax.random.fold_in(own, 3), count)
    giver, sink = mixed[0:count // 2 * 2:2], mixed[1:count // 2 * 2:2]
    margin = jnp.minimum(lengths[giver] - 1, reach - lengths[sink]) // 2
    margin = jnp.where((giver == order[0]) | (sink == order[0]) | (lengths[sink] == 0), 0, jnp.maximum(margin, 0))
    passed = jax.random.randint(jax.random.fold_in(own, 4), (count // 2,), 0, 1 << 20) % (margin + 1)
    lengths = lengths.at[giver].add(-passed).at[sink].add(passed)
    items = jnp.searchsorted(jnp.cumsum(lengths), jnp.arange(rows * top), side="right").astype(jnp.int32)
    grid = items.reshape(top, rows).T
    grid = grid[jax.random.permutation(jax.random.fold_in(own, 1), rows)]
    turn = jax.random.randint(jax.random.fold_in(own, 2), (rows, 1), 0, top)
    return jnp.take_along_axis(grid, (jnp.arange(top)[None, :] + turn) % top, axis=1)


def load_shares(number_of, total, bound, skew, full):
    weights = [(1 << 20) // math.isqrt(standing ** skew) + 1 for standing in range(1, number_of + 1)]
    largest = bound if full else min(bound, max(-(-total // number_of), total * weights[0] // sum(weights)))
    least = 1 if total - largest >= number_of - 1 else 0
    given, rest = [largest] + [least] * (number_of - 1), total - largest - least * (number_of - 1)
    while rest > 0:
        free = [i for i in range(1, number_of) if given[i] < largest] or [i for i in range(1, number_of) if given[i] < bound]
        pool, budget = sum([weights[i] for i in free]), rest
        for i in free:
            addition = min(bound - given[i], max(1, budget * weights[i] // pool), rest)
            given[i] = given[i] + addition
            rest = rest - addition
    return np.array(given)


def noise(key, extent, spread, most, cuts=(), kind=jnp.bfloat16):
    entries = spread * jax.random.normal(key, extent, jnp.float32)
    if cuts:
        entries = entries * levels(key, extent, cuts, -0.22, 0.18)
    return jnp.clip(entries, -most, most).astype(kind)


def setup_inputs(seed: int = 0) -> dict:
    splits = jax.random.split(jax.random.key(seed), 9)
    residual = noise(splits[0], (TOKENS, D), 1.0, 6.0, ((0, 1024),))
    expert_hidden = noise(splits[1], (N_DP * EXPERTS, N_TENSOR * CAP, FF), 1.0, 6.0, ((0, 1024),))
    down_weight = noise(splits[2], (EXPERTS, FF, D), FF ** -0.5, 0.21875, ((0, 16),))
    gates = jnp.clip(0.1 + 0.79999997 * jax.random.uniform(splits[3], (TOKENS, TOP), jnp.float32) ** levels(splits[3], (TOKENS, TOP), ((0, 1024),), -0.2, 0.2), 0.1, 0.9)
    routes_keys = jax.random.split(jax.random.fold_in(splits[4], 1), TOKENS // TOK_DEV)
    routes_turns = jax.random.permutation(jax.random.fold_in(splits[4], 3), TOKENS // TOK_DEV)
    routes = jax.vmap(lambda own, number: shared_out(jax.random.fold_in(splits[4], 2), own, number, TOK_DEV, EXPERTS, TOP, CAP, 2))(routes_keys, routes_turns).reshape((TOKENS, TOP))
    router_probs = draw_router_probs(jax.random.fold_in(splits[8], 71), 0)
    norm_gain = jnp.clip(1.0 + 0.1 * jax.random.normal(splits[6], (D,), jnp.float32), 0.5, 1.5)
    qkv_weight = noise(splits[7], (D, QKVC), D ** -0.5, 0.09375, ((1, 16),))
    return {"residual": residual, "expert_hidden": expert_hidden, "down_weight": down_weight, "gates": gates, "routes": routes, "router_probs": router_probs, "norm_gain": norm_gain, "qkv_weight": qkv_weight}


eps = 1e-06

def normalize(rows, norm_gain):
    values = rows.astype(jnp.float32)
    scale = lax.rsqrt(lax.optimization_barrier(jnp.mean(values * values, axis=-1, keepdims=True)) + eps)
    return (values * scale * norm_gain).astype(jnp.bfloat16)

def slot_ranks(routes):
    blocks = routes.reshape(-1, TOK_DEV * TOP)
    labels = jnp.arange(EXPERTS, dtype=jnp.int32)
    onehot = (blocks[:, :, None] == labels[None, None, :]).astype(jnp.int32)
    before = jnp.cumsum(onehot, axis=1) - onehot
    return lax.optimization_barrier(jnp.sum(before * onehot, axis=2)).astype(jnp.int32).reshape(TOKENS, TOP)

def reference(residual, expert_hidden, down_weight, gates, routes, router_probs, norm_gain, qkv_weight):
    slot_rank = slot_ranks(routes)
    source = jnp.arange(GROUP, dtype=jnp.int32) // TOK_DEV
    down_wide = down_weight.astype(jnp.float32)

    def one_group(packed):
        hidden_block, route_block, rank_block, gate_block, residual_block = packed
        outputs = jnp.einsum('erf,efd->erd', hidden_block.astype(jnp.float32), down_wide).astype(jnp.bfloat16)
        outputs = outputs.reshape(EXPERTS * EXPERTS * CAP, D)
        row_index = (route_block * (EXPERTS * CAP) + source[:, None] * CAP + rank_block).astype(jnp.int32)
        picked = outputs[row_index].astype(jnp.float32)
        mixture = lax.optimization_barrier(jnp.sum(gate_block[:, :, None] * picked, axis=1))
        fresh = (residual_block.astype(jnp.float32) + mixture).astype(jnp.bfloat16)
        normed = normalize(fresh, norm_gain)
        projected = jnp.dot(normed, qkv_weight, preferred_element_type=jnp.float32).astype(jnp.bfloat16)
        return (fresh, projected)
    packed = (expert_hidden.reshape(N_DP, EXPERTS, EXPERTS * CAP, FF), routes.reshape(N_DP, GROUP, TOP), slot_rank.reshape(N_DP, GROUP, TOP), gates.reshape(N_DP, GROUP, TOP), residual.reshape(N_DP, GROUP, D))
    fresh, projected = lax.map(one_group, packed)
    labels = jnp.arange(EXPERTS, dtype=jnp.int32)
    onehot = (routes[:, :, None] == labels[None, None, :]).astype(jnp.float32)
    usage = lax.optimization_barrier(jnp.sum(onehot, axis=(0, 1))) / (TOKENS * TOP)
    shares = lax.optimization_barrier(jnp.sum(router_probs, axis=0)) / TOKENS
    balance = EXPERTS * jnp.sum(usage * shares)
    return (fresh.reshape(TOKENS, D), projected.reshape(TOKENS, QKVC), balance)
```

```python
import jax
import jax.numpy as jnp
from jax import lax
from jax.experimental import pallas as pl
from jax.experimental.pallas import tpu as pltpu
from jax.sharding import PartitionSpec as P

eps = 1e-06


def expert_kernel(hidden_ref, weight_ref, routes_ref, probs_ref, out_ref, counts_ref, shares_ref):
    out_ref[...] = jnp.dot(
        hidden_ref[...], weight_ref[...], preferred_element_type=jnp.float32
    ).astype(jnp.bfloat16)

    @pl.when(pl.program_id(0) == 0)
    def _():
        routes = routes_ref[...]
        rows, experts = probs_ref.shape
        label = lax.broadcasted_iota(jnp.int32, (rows, experts), 1)
        named = jnp.where(label == routes[:, 0:1], 1.0, 0.0)
        for j in range(1, routes.shape[1]):
            named = named + jnp.where(label == routes[:, j : j + 1], 1.0, 0.0)
        counts_ref[...] = jnp.sum(named, axis=0, keepdims=True)
        shares_ref[...] = jnp.sum(probs_ref[...], axis=0, keepdims=True)


def expert_project(hidden, weight, routes, probs, steps=4):
    slots, depth = hidden.shape
    width = weight.shape[1]
    block = width // steps
    whole = lambda shape: pl.BlockSpec(shape, lambda i: (0, 0))
    return pl.pallas_call(
        expert_kernel,
        grid=(steps,),
        in_specs=[
            whole(hidden.shape),
            pl.BlockSpec((depth, block), lambda i: (0, i)),
            whole(routes.shape),
            whole(probs.shape),
        ],
        out_specs=[
            pl.BlockSpec((slots, block), lambda i: (0, i)),
            whole((1, probs.shape[1])),
            whole((1, probs.shape[1])),
        ],
        out_shape=[
            jax.ShapeDtypeStruct((slots, width), jnp.bfloat16),
            jax.ShapeDtypeStruct((1, probs.shape[1]), jnp.float32),
            jax.ShapeDtypeStruct((1, probs.shape[1]), jnp.float32),
        ],
        compiler_params=pltpu.CompilerParams(vmem_limit_bytes=56 * 2**20),
        cost_estimate=pl.CostEstimate(
            flops=2 * slots * depth * width,
            bytes_accessed=2 * (depth * width + slots * (depth + width)),
            transcendentals=0,
        ),
        name="expert_project",
    )(hidden, weight, routes, probs)


def pick_kernel(slot_count, routes_ref, gates_ref, high_ref, low_ref):
    rows, columns = high_ref.shape
    lane = lax.broadcasted_iota(jnp.int32, (rows, columns), 1)
    expert = lax.shift_right_logical(lane, slot_count.bit_length() - 1)
    slot = (lane & (slot_count - 1)).astype(jnp.float32)
    named = jnp.zeros((rows, columns), jnp.float32)
    gate = jnp.zeros((rows, columns), jnp.float32)
    for j in range(routes_ref.shape[1]):
        hit = expert == routes_ref[:, j : j + 1]
        named = named + jnp.where(hit, 1.0, 0.0)
        gate = gate + jnp.where(hit, gates_ref[:, j : j + 1], 0.0)
    row = lax.broadcasted_iota(jnp.int32, (rows, rows), 0)
    column = lax.broadcasted_iota(jnp.int32, (rows, rows), 1)
    earlier = jnp.where(column < row, 1.0, 0.0).astype(jnp.bfloat16)
    rank = jnp.dot(earlier, named.astype(jnp.bfloat16), preferred_element_type=jnp.float32)
    pick = jnp.where(rank == slot, gate, 0.0)
    high = pick.astype(jnp.bfloat16)
    high_ref[...] = high
    low_ref[...] = (pick - high.astype(jnp.float32)).astype(jnp.bfloat16)


def pick_matrix(routes, gates, columns, slot_count):
    rows = routes.shape[0]
    shape = jax.ShapeDtypeStruct((rows, columns), jnp.bfloat16)
    return pl.pallas_call(
        lambda *refs: pick_kernel(slot_count, *refs),
        out_shape=[shape, shape],
        name="pick_matrix",
    )(routes, gates)


def combine_kernel(
    high_ref,
    low_ref,
    slots_ref,
    residual_ref,
    gain_ref,
    counts_ref,
    shares_ref,
    fresh_ref,
    normed_ref,
    counts_out_ref,
    shares_out_ref,
):
    rows, width = residual_ref.shape
    counts_out_ref[...] = counts_ref[...]
    shares_out_ref[...] = shares_ref[...]
    pick = jnp.concatenate([high_ref[...], low_ref[...]], axis=0)
    block = 512
    total = jnp.zeros((rows, 128), jnp.float32)
    for start in range(0, width, block):
        at = pl.ds(start, block)
        both = jnp.dot(pick, slots_ref[:, at], preferred_element_type=jnp.float32)
        mixture = both[:rows] + both[rows:]
        fresh = (residual_ref[:, at].astype(jnp.float32) + mixture).astype(jnp.bfloat16)
        fresh_ref[:, at] = fresh
        values = fresh.astype(jnp.float32)
        square = values * values
        for lane in range(0, block, 128):
            total = total + square[:, lane : lane + 128]
    mean = jnp.sum(total, axis=1, keepdims=True) / width
    scale = lax.rsqrt(mean + eps)
    for start in range(0, width, block):
        at = pl.ds(start, block)
        values = fresh_ref[:, at].astype(jnp.float32)
        normed_ref[:, at] = (values * scale * gain_ref[:, at]).astype(jnp.bfloat16)


def combine(high, low, slots, residual, gain, counts, shares):
    rows, width = residual.shape
    return pl.pallas_call(
        combine_kernel,
        out_shape=[
            jax.ShapeDtypeStruct((rows, width), jnp.bfloat16),
            jax.ShapeDtypeStruct((rows, width), jnp.bfloat16),
            jax.ShapeDtypeStruct(counts.shape, jnp.float32),
            jax.ShapeDtypeStruct(shares.shape, jnp.float32),
        ],
        compiler_params=pltpu.CompilerParams(vmem_limit_bytes=16 * 2**20),
        cost_estimate=pl.CostEstimate(
            flops=4 * rows * slots.shape[0] * width,
            bytes_accessed=2 * (slots.size + 3 * residual.size),
            transcendentals=0,
        ),
        name="combine_and_norm",
    )(high, low, slots, residual, gain, counts, shares)


def project_kernel(weight_ref, rows_ref, out_ref):
    out_ref[...] = lax.dot_general(
        weight_ref[...],
        rows_ref[...],
        (((1,), (1,)), ((), ())),
        preferred_element_type=jnp.float32,
    ).astype(jnp.bfloat16)


def project(rows, weight_t, block=256):
    count, width = rows.shape
    columns = weight_t.shape[0]
    return pl.pallas_call(
        project_kernel,
        grid=(count // block,),
        in_specs=[
            pl.BlockSpec((columns, width), lambda i: (0, 0)),
            pl.BlockSpec((block, width), lambda i: (i, 0)),
        ],
        out_specs=pl.BlockSpec((columns, block), lambda i: (0, i)),
        out_shape=jax.ShapeDtypeStruct((columns, count), jnp.bfloat16),
        compiler_params=pltpu.CompilerParams(vmem_limit_bytes=56 * 2**20),
        cost_estimate=pl.CostEstimate(
            flops=2 * count * width * columns,
            bytes_accessed=2 * (count * width + columns * (width + count)),
            transcendentals=0,
        ),
        name="qkv_project",
    )(weight_t, rows)


def on_device(
    residual, expert_hidden, down_weight, gates, routes, router_probs, norm_gain, qkv_weight
):
    experts = lax.axis_size("tensor")
    rows_dev, width = residual.shape
    top_count = routes.shape[1]
    slot_count = expert_hidden.shape[1] // experts
    expert_out, counts, shares = expert_project(
        expert_hidden[0], down_weight[0], routes, router_probs
    )
    returned = lax.all_to_all(
        expert_out.reshape(experts, slot_count, width),
        "tensor",
        split_axis=0,
        concat_axis=0,
        tiled=True,
    ).reshape(experts * slot_count, width)
    depth = 16
    breadth = lax.axis_size("dp") // depth
    lines = [[x * depth + z for z in range(depth)] for x in range(breadth)]
    cross = [[x * depth + z for x in range(breadth)] for z in range(depth)]
    sums = lax.psum((counts, shares), "dp", axis_index_groups=cross)
    sums = lax.psum(sums, "dp", axis_index_groups=lines)
    high, low = pick_matrix(routes, gates, experts * slot_count, slot_count)
    fresh, normed, counts, shares = combine(
        high, low, returned, residual, norm_gain.reshape(1, width), *sums
    )
    gathered = lax.all_gather(normed, "tensor", axis=0, tiled=True)
    totals = lax.psum((counts, shares), "tensor")
    total_tokens = rows_dev * lax.axis_size("dp") * experts
    usage = totals[0] / (total_tokens * top_count)
    share_mean = totals[1] / total_tokens
    balance = experts * jnp.sum(usage * share_mean)
    projected = project(gathered, qkv_weight.T).T
    return (fresh, projected, balance)


def solution(mesh):
    in_specs = (
        P(("dp", "tensor"), None),
        P(("dp", "tensor"), None, None),
        P("tensor", None, None),
        P(("dp", "tensor"), None),
        P(("dp", "tensor"), None),
        P(("dp", "tensor"), None),
        P(),
        P(None, "tensor"),
    )
    out_specs = (P(("dp", "tensor"), None), P("dp", "tensor"), P())
    return jax.shard_map(
        on_device, mesh=mesh, in_specs=in_specs, out_specs=out_specs, check_vma=False
    )
```

```python
import jax
import jax.numpy as jnp
from jax import lax
from jax.experimental import pallas as pl
from jax.experimental.pallas import tpu as pltpu
from jax.sharding import PartitionSpec as P

eps = 1e-06
lanes = 128
MIB = 2**20


def expert_kernel(hidden_ref, *refs):
    weight_refs, out_ref = refs[:-1], refs[-1]
    depth = weight_refs[0].shape[0]
    total = None
    for k, weight_ref in enumerate(weight_refs):
        part = jnp.dot(
            hidden_ref[:, k * depth : (k + 1) * depth],
            weight_ref[...],
            preferred_element_type=jnp.float32,
        )
        total = part if total is None else total + part
    out_ref[...] = total.astype(jnp.bfloat16)


def expert_project(hidden, weight, steps=2, parts=1):
    slots, depth = hidden.shape
    width = weight.shape[1]
    block = width // steps
    weight_spec = lambda k: pl.BlockSpec((depth // parts, block), lambda i: (k, i))
    return pl.pallas_call(
        expert_kernel,
        grid=(steps,),
        in_specs=[pl.BlockSpec((slots, depth), lambda i: (0, 0))]
        + [weight_spec(k) for k in range(parts)],
        out_specs=pl.BlockSpec((slots, block), lambda i: (0, i)),
        out_shape=jax.ShapeDtypeStruct((slots, width), jnp.bfloat16),
        compiler_params=pltpu.CompilerParams(vmem_limit_bytes=56 * MIB),
        cost_estimate=pl.CostEstimate(
            flops=2 * slots * depth * width,
            bytes_accessed=2 * (depth * width + slots * (depth + width)),
            transcendentals=0,
        ),
        name="expert_project",
    )(hidden, *([weight] * parts))


def pick_kernel(slot_count, routes_ref, gates_ref, probs_ref, pick_ref, counts_ref, shares_ref):
    top_count, rows = routes_ref.shape
    experts = probs_ref.shape[0]
    count = experts * slot_count
    place = lax.broadcasted_iota(jnp.int32, (count, rows), 0)
    expert = lax.shift_right_logical(place, slot_count.bit_length() - 1)
    slot = (place & (slot_count - 1)).astype(jnp.float32)
    label = lax.broadcasted_iota(jnp.int32, (experts, rows), 0)
    named = jnp.zeros((count, rows), jnp.float32)
    gate = jnp.zeros((count, rows), jnp.float32)
    chosen = jnp.zeros((experts, rows), jnp.float32)
    for j in range(top_count):
        route = routes_ref[j : j + 1, :]
        hit = expert == route
        named = named + jnp.where(hit, 1.0, 0.0)
        gate = gate + jnp.where(hit, gates_ref[j : j + 1, :], 0.0)
        chosen = chosen + jnp.where(label == route, 1.0, 0.0)
    row = lax.broadcasted_iota(jnp.int32, (rows, rows), 0)
    column = lax.broadcasted_iota(jnp.int32, (rows, rows), 1)
    earlier = jnp.where(row < column, 1.0, 0.0).astype(jnp.bfloat16)
    rank = jnp.dot(named.astype(jnp.bfloat16), earlier, preferred_element_type=jnp.float32)
    pick = jnp.where(rank == slot, gate, 0.0)
    high = pick.astype(jnp.bfloat16)
    low = (pick - high.astype(jnp.float32)).astype(jnp.bfloat16)
    pick_ref[...] = jnp.concatenate([high, low], axis=1)
    for sums_ref, values in ((counts_ref, chosen), (shares_ref, probs_ref[...])):
        sums = lax.dot_general(
            jnp.ones((8, rows), jnp.float32),
            values,
            (((1,), (1,)), ((), ())),
            precision=lax.Precision.HIGHEST,
            preferred_element_type=jnp.float32,
        )
        sums_ref[...] = sums[0:1]


def pick_matrix(routes, gates, probs, slot_count):
    experts, rows = probs.shape
    sums = jax.ShapeDtypeStruct((1, experts), jnp.float32)
    return pl.pallas_call(
        lambda *refs: pick_kernel(slot_count, *refs),
        out_shape=[
            jax.ShapeDtypeStruct((experts * slot_count, 2 * rows), jnp.bfloat16),
            sums,
            sums,
        ],
        compiler_params=pltpu.CompilerParams(vmem_limit_bytes=8 * MIB),
        name="pick_matrix",
    )(routes, gates, probs)


def combine_kernel(
    pick_ref,
    slots_ref,
    residual_ref,
    gain_ref,
    counts_ref,
    shares_ref,
    fresh_ref,
    normed_ref,
    ring_ref,
):
    rows, width = residual_ref.shape
    split = normed_ref.shape[1]
    block = 256
    total = jnp.zeros((rows, lanes), jnp.float32)
    pick = pick_ref[...]
    for start in range(0, width, block):
        at = pl.ds(start, block)
        both = lax.dot_general(
            pick,
            slots_ref[:, at],
            (((0,), (0,)), ((), ())),
            preferred_element_type=jnp.float32,
        )
        mixture = both[:rows] + both[rows:]
        fresh = (residual_ref[:, at].astype(jnp.float32) + mixture).astype(jnp.bfloat16)
        fresh_ref[:, at] = fresh
        values = fresh.astype(jnp.float32)
        square = values * values
        for lane in range(0, block, lanes):
            total = total + square[:, lane : lane + lanes]
    mean = jnp.sum(total, axis=1, keepdims=True) / width
    scale = lax.rsqrt(mean + eps)
    for start in range(0, width, block):
        at = pl.ds(start, block)
        values = fresh_ref[:, at].astype(jnp.float32)
        normed = (values * scale * gain_ref[:, at]).astype(jnp.bfloat16)
        if start < split:
            normed_ref[:, at] = normed
        else:
            ring_ref[:, pl.ds(start - split, block)] = normed
    row = lax.broadcasted_iota(jnp.int32, (rows, lanes), 0)
    riding = jnp.zeros((rows, lanes), jnp.float32)
    pad = jnp.zeros((1, lanes - counts_ref.shape[1]), jnp.float32)
    for base, ref in ((0, counts_ref), (3, shares_ref)):
        rest = jnp.concatenate([ref[...], pad], axis=1)
        for part in range(3):
            piece = rest.astype(jnp.bfloat16).astype(jnp.float32)
            rest = rest - piece
            riding = jnp.where(row == base + part, piece, riding)
    ring_ref[:, pl.ds(width - split, lanes)] = riding.astype(jnp.bfloat16)


def combine(pick, slots, residual, gain, counts, shares, split):
    rows, width = residual.shape
    return pl.pallas_call(
        combine_kernel,
        out_shape=[
            jax.ShapeDtypeStruct((rows, width), jnp.bfloat16),
            jax.ShapeDtypeStruct((rows, split), jnp.bfloat16),
            jax.ShapeDtypeStruct((rows, width - split + lanes), jnp.bfloat16),
        ],
        compiler_params=pltpu.CompilerParams(vmem_limit_bytes=16 * MIB),
        cost_estimate=pl.CostEstimate(
            flops=4 * rows * slots.shape[0] * width,
            bytes_accessed=2 * (slots.size + 3 * residual.size),
            transcendentals=0,
        ),
        name="combine_and_norm",
    )(pick, slots, residual, gain, counts, shares)


def ring_kernel(
    rows, factors, me_ref, weight_ref, own_ref, other_ref, sums_ref, balance_ref, held_ref
):
    chips = own_ref.shape[0] // rows
    share = own_ref.shape[1] - lanes
    chip = lax.shift_right_logical(me_ref[0], 1)
    first = (me_ref[0] & 1) == 0
    for step in range(chips):
        own = own_ref[step * rows : (step + 1) * rows, :]
        other = other_ref[step * rows : (step + 1) * rows, :]
        source = lax.rem(chip - step + chips, chips)
        pair = jnp.concatenate([jnp.where(first, own, other), jnp.where(first, other, own)], axis=0)
        held_ref[pl.ds(pl.multiple_of(source * 2 * rows, 2 * rows), 2 * rows), :] = pair
    sums_ref[...] = lax.dot_general(
        weight_ref[:, pl.ds(weight_ref.shape[1] - share, share)],
        held_ref[:, pl.ds(0, share)],
        (((1,), (1,)), ((), ())),
        preferred_element_type=jnp.float32,
    )
    riding = jnp.zeros((16, lanes), jnp.float32)
    for source in range(2 * chips):
        riding = riding + held_ref[pl.ds(source * rows, 16), pl.ds(share, lanes)].astype(jnp.float32)
    tokens_of, pairs_of, experts = factors
    usage = (riding[0:1] + riding[1:2] + riding[2:3]) / pairs_of
    shares = (riding[3:4] + riding[4:5] + riding[5:6]) / tokens_of
    balance_ref[...] = experts * jnp.sum(usage * shares, axis=1, keepdims=True)


def ring_project(me, weight_t, own, other, rows, factors):
    columns, width = weight_t.shape
    count, share = 2 * own.shape[0], own.shape[1] - lanes
    vmem = pl.BlockSpec(memory_space=pltpu.VMEM)
    return pl.pallas_call(
        lambda *refs: ring_kernel(rows, factors, *refs),
        in_specs=[pl.BlockSpec(memory_space=pltpu.SMEM), vmem, vmem, vmem],
        out_specs=[vmem, vmem],
        out_shape=[
            jax.ShapeDtypeStruct((columns, count), jnp.float32),
            jax.ShapeDtypeStruct((1, 1), jnp.float32),
        ],
        scratch_shapes=[pltpu.VMEM((count, own.shape[1]), jnp.bfloat16)],
        compiler_params=pltpu.CompilerParams(vmem_limit_bytes=24 * MIB),
        cost_estimate=pl.CostEstimate(
            flops=2 * count * share * columns,
            bytes_accessed=2 * (count * share + columns * (width + 2 * count)),
            transcendentals=0,
        ),
        name="ring_project",
    )(me, weight_t, own, other)


def project_kernel(weight_ref, rows_ref, sums_ref, out_ref):
    product = lax.dot_general(
        weight_ref[...],
        rows_ref[...],
        (((1,), (1,)), ((), ())),
        preferred_element_type=jnp.float32,
    )
    out_ref[...] = (product + sums_ref[...]).astype(jnp.bfloat16)


def project(weight_t, gathered, sums, steps=2):
    count, share = gathered.shape
    columns = weight_t.shape[0]
    block = count // steps
    return pl.pallas_call(
        project_kernel,
        grid=(steps,),
        in_specs=[
            pl.BlockSpec((columns, share), lambda i: (0, 0)),
            pl.BlockSpec((block, share), lambda i: (i, 0)),
            pl.BlockSpec((columns, block), lambda i: (0, i)),
        ],
        out_specs=pl.BlockSpec((columns, block), lambda i: (0, i)),
        out_shape=jax.ShapeDtypeStruct((columns, count), jnp.bfloat16),
        compiler_params=pltpu.CompilerParams(vmem_limit_bytes=56 * MIB),
        cost_estimate=pl.CostEstimate(
            flops=2 * count * share * columns,
            bytes_accessed=2 * (count * share + columns * (share + 3 * count)),
            transcendentals=0,
        ),
        name="qkv_project",
    )(weight_t, gathered, sums)


def on_device(
    residual, expert_hidden, down_weight, gates, routes, router_probs, norm_gain, qkv_weight
):
    experts = lax.axis_size("tensor")
    rows, width = residual.shape
    slot_count = expert_hidden.shape[1] // experts
    split = width * 3 // 4
    expert_out = expert_project(expert_hidden[0], down_weight[0])
    returned = lax.all_to_all(
        expert_out.reshape(experts, slot_count, width),
        "tensor",
        split_axis=0,
        concat_axis=0,
        tiled=True,
    ).reshape(experts * slot_count, width)
    pick, counts, shares = pick_matrix(routes.T, gates.T, router_probs.T, slot_count)
    depth = 16
    breadth = lax.axis_size("dp") // depth
    lines = [[x * depth + z for z in range(depth)] for x in range(breadth)]
    cross = [[x * depth + z for x in range(breadth)] for z in range(depth)]
    sums = lax.psum((counts, shares), "dp", axis_index_groups=cross)
    sums = lax.psum(sums, "dp", axis_index_groups=lines)
    fresh, normed, riding = combine(
        pick, returned, residual, norm_gain.reshape(1, width), *sums, split
    )
    gathered = lax.all_gather(normed, "tensor", axis=0, tiled=True)
    chips = experts // 2
    up = [(i, (i + 2) % experts) for i in range(experts)]
    down = [(i, (i - 2) % experts) for i in range(experts)]
    ups, downs = [riding], [riding]
    for step in range(chips // 2):
        ups.append(lax.ppermute(ups[-1], "tensor", up))
        if step < chips // 2 - 1:
            downs.append(lax.ppermute(downs[-1], "tensor", down))
    own = jnp.concatenate(ups + downs[:0:-1], axis=0)
    other = lax.ppermute(own, "tensor", [(i, i ^ 1) for i in range(experts)])
    total_tokens = rows * lax.axis_size("dp") * experts
    factors = (float(total_tokens), float(total_tokens * routes.shape[1]), float(experts))
    me = lax.axis_index("tensor").astype(jnp.int32).reshape(1)
    weight_t = qkv_weight.T
    part, balance = ring_project(me, weight_t, own, other, rows, factors)
    projected = project(weight_t, gathered, part).T
    return (fresh, projected, balance.reshape(()))


def solution(mesh):
    in_specs = (
        P(("dp", "tensor"), None),
        P(("dp", "tensor"), None, None),
        P("tensor", None, None),
        P(("dp", "tensor"), None),
        P(("dp", "tensor"), None),
        P(("dp", "tensor"), None),
        P(),
        P(None, "tensor"),
    )
    out_specs = (P(("dp", "tensor"), None), P("dp", "tensor"), P())
    return jax.shard_map(
        on_device, mesh=mesh, in_specs=in_specs, out_specs=out_specs, check_vma=False
    )
```

```python
import jax
import jax.numpy as jnp
from jax import lax
from jax.experimental import pallas as pl
from jax.experimental.pallas import tpu as pltpu
from jax.sharding import PartitionSpec as P

eps = 1e-06
lanes = 128
scale_lane = 64
MIB = 2**20


def expert_kernel(hidden_ref, weight_ref, out_ref):
    out_ref[...] = jnp.dot(
        hidden_ref[...], weight_ref[...], preferred_element_type=jnp.float32
    ).astype(jnp.bfloat16)


def expert_project(hidden, weight, start, width, steps):
    slots, depth = hidden.shape
    block = width // steps
    return pl.pallas_call(
        expert_kernel,
        grid=(steps,),
        in_specs=[
            pl.BlockSpec((slots, depth), lambda i: (0, 0)),
            pl.BlockSpec((depth, block), lambda i: (0, start // block + i)),
        ],
        out_specs=pl.BlockSpec((slots, block), lambda i: (0, i)),
        out_shape=jax.ShapeDtypeStruct((slots, width), jnp.bfloat16),
        compiler_params=pltpu.CompilerParams(vmem_limit_bytes=56 * MIB),
        cost_estimate=pl.CostEstimate(
            flops=2 * slots * depth * width,
            bytes_accessed=2 * (depth * width + slots * (depth + width)),
            transcendentals=0,
        ),
        name="expert_project",
    )(hidden, weight)


def pick_kernel(
    slot_count, routes_ref, gates_ref, probs_ref, _, pick_ref, sums_ref
):
    top_count, rows = routes_ref.shape
    experts = probs_ref.shape[0]
    count = experts * slot_count
    place = lax.broadcasted_iota(jnp.int32, (count, rows), 0)
    expert = lax.shift_right_logical(place, slot_count.bit_length() - 1)
    slot = (place & (slot_count - 1)).astype(jnp.float32)
    label = lax.broadcasted_iota(jnp.int32, (experts, rows), 0)
    named = jnp.zeros((count, rows), jnp.float32)
    gate = jnp.zeros((count, rows), jnp.float32)
    chosen = jnp.zeros((experts, rows), jnp.float32)
    for j in range(top_count):
        route = routes_ref[j : j + 1, :]
        hit = expert == route
        named = named + jnp.where(hit, 1.0, 0.0)
        gate = gate + jnp.where(hit, gates_ref[j : j + 1, :], 0.0)
        chosen = chosen + jnp.where(label == route, 1.0, 0.0)
    row = lax.broadcasted_iota(jnp.int32, (rows, rows), 0)
    column = lax.broadcasted_iota(jnp.int32, (rows, rows), 1)
    earlier = jnp.where(row < column, 1.0, 0.0).astype(jnp.bfloat16)
    rank = jnp.dot(named.astype(jnp.bfloat16), earlier, preferred_element_type=jnp.float32)
    pick = jnp.where(rank == slot, gate, 0.0)
    high = pick.astype(jnp.bfloat16)
    low = (pick - high.astype(jnp.float32)).astype(jnp.bfloat16)
    pick_ref[...] = jnp.concatenate([high, low], axis=1)
    for place, values in enumerate((chosen, probs_ref[...])):
        sums = lax.dot_general(
            jnp.ones((8, rows), jnp.float32),
            values,
            (((1,), (1,)), ((), ())),
            precision=lax.Precision.HIGHEST,
            preferred_element_type=jnp.float32,
        )
        sums_ref[place : place + 1, :] = sums[0:1]


def pick_matrix(routes, gates, probs, before, slot_count):
    experts, rows = probs.shape
    return pl.pallas_call(
        lambda *refs: pick_kernel(slot_count, *refs),
        in_specs=[pl.BlockSpec(memory_space=pltpu.VMEM)] * 3
        + [pl.BlockSpec(memory_space=pl.ANY)],
        out_shape=[
            jax.ShapeDtypeStruct((experts * slot_count, 2 * rows), jnp.bfloat16),
            jax.ShapeDtypeStruct((2, experts), jnp.float32),
        ],
        compiler_params=pltpu.CompilerParams(vmem_limit_bytes=8 * MIB),
        name="pick_matrix",
    )(routes, gates, probs, before)


def combine_block(pick_ref, slots_ref, residual_ref, gain_ref, start, at, block):
    rows = residual_ref.shape[0]
    both = lax.dot_general(
        pick_ref[...],
        slots_ref[:, pl.ds(at, block)],
        (((0,), (0,)), ((), ())),
        preferred_element_type=jnp.float32,
    )
    mixture = both[:rows] + both[rows:]
    columns = pl.ds(start + at, block)
    fresh = (residual_ref[:, columns].astype(jnp.float32) + mixture).astype(jnp.bfloat16)
    values = fresh.astype(jnp.float32)
    scaled = (values * gain_ref[:, columns]).astype(jnp.bfloat16)
    return fresh, scaled


def first_kernel(
    pick_ref, slots_ref, residual_ref, gain_ref, sums_ref, head_ref, scaled_ref, sums_out_ref
):
    sums_out_ref[...] = sums_ref[...]
    block = 256
    split, width = scaled_ref.shape[1], residual_ref.shape[1]
    for at in range(0, split, block):
        fresh, scaled = combine_block(pick_ref, slots_ref, residual_ref, gain_ref, 0, at, block)
        head_ref[:, pl.ds(at, block)] = fresh
        scaled_ref[:, pl.ds(at, block)] = scaled
    head_ref[:, pl.ds(split, width - split)] = residual_ref[:, pl.ds(split, width - split)]


def combine_first(pick, slots, residual, gain, sums):
    rows, width = residual.shape
    split = slots.shape[1]
    return pl.pallas_call(
        first_kernel,
        out_shape=[
            jax.ShapeDtypeStruct((rows, width), jnp.bfloat16),
            jax.ShapeDtypeStruct((rows, split), jnp.bfloat16),
            jax.ShapeDtypeStruct(sums.shape, jnp.float32),
        ],
        compiler_params=pltpu.CompilerParams(vmem_limit_bytes=16 * MIB),
        cost_estimate=pl.CostEstimate(
            flops=4 * rows * slots.shape[0] * split,
            bytes_accessed=2 * (slots.size + 3 * rows * width),
            transcendentals=0,
        ),
        name="combine_first",
    )(pick, slots, residual, gain, sums)


def last_kernel(pick_ref, slots_ref, head_ref, gain_ref, sums_ref, fresh_ref, ring_ref):
    rows, width = head_ref.shape
    share = slots_ref.shape[1]
    split = width - share
    block = 256
    total = jnp.zeros((rows, lanes), jnp.float32)
    for start in range(0, width, block):
        columns = pl.ds(start, block)
        if start < split:
            fresh = head_ref[:, columns]
        else:
            at = start - split
            fresh, scaled = combine_block(
                pick_ref, slots_ref, head_ref, gain_ref, split, at, block
            )
            ring_ref[:, pl.ds(at, block)] = scaled
        fresh_ref[:, columns] = fresh
        values = fresh.astype(jnp.float32)
        square = values * values
        for lane in range(0, block, lanes):
            total = total + square[:, lane : lane + lanes]
    mean = jnp.sum(total, axis=1, keepdims=True) / width
    scale = lax.rsqrt(mean + eps)
    row = lax.broadcasted_iota(jnp.int32, (rows, lanes), 0)
    lane = lax.broadcasted_iota(jnp.int32, (rows, lanes), 1)
    riding = jnp.zeros((rows, lanes), jnp.float32)
    pad = jnp.zeros((1, lanes - sums_ref.shape[1]), jnp.float32)
    for place in range(2):
        rest = jnp.concatenate([sums_ref[place : place + 1, :], pad], axis=1)
        for part in range(3):
            piece = rest.astype(jnp.bfloat16).astype(jnp.float32)
            rest = rest - piece
            riding = jnp.where(row == 3 * place + part, piece, riding)
    rest = scale
    for part in range(3):
        piece = rest.astype(jnp.bfloat16).astype(jnp.float32)
        rest = rest - piece
        riding = jnp.where(lane == scale_lane + part, piece, riding)
    ring_ref[:, pl.ds(share, lanes)] = riding.astype(jnp.bfloat16)


def combine_last(pick, slots, head, gain, sums):
    rows, width = head.shape
    share = slots.shape[1]
    return pl.pallas_call(
        last_kernel,
        out_shape=[
            jax.ShapeDtypeStruct((rows, width), jnp.bfloat16),
            jax.ShapeDtypeStruct((rows, share + lanes), jnp.bfloat16),
        ],
        compiler_params=pltpu.CompilerParams(vmem_limit_bytes=16 * MIB),
        cost_estimate=pl.CostEstimate(
            flops=4 * rows * slots.shape[0] * share,
            bytes_accessed=2 * (slots.size + 3 * rows * width),
            transcendentals=0,
        ),
        name="combine_last",
    )(pick, slots, head, gain, sums)


def stack_kernel(*refs):
    out_ref = refs[-1]
    rows = refs[0].shape[0]
    for place, ref in enumerate(refs[:-1]):
        out_ref[pl.ds(place * rows, rows), :] = ref[...]


def stack(blocks):
    rows, columns = blocks[0].shape
    return pl.pallas_call(
        stack_kernel,
        out_shape=jax.ShapeDtypeStruct((len(blocks) * rows, columns), jnp.bfloat16),
        compiler_params=pltpu.CompilerParams(vmem_limit_bytes=16 * MIB),
        name="stack_blocks",
    )(*blocks)


def ring_kernel(
    rows,
    factors,
    me_ref,
    weight_ref,
    own_ref,
    other_ref,
    sums_ref,
    scale_ref,
    balance_ref,
    held_ref,
):
    chips = own_ref.shape[0] // rows
    share = own_ref.shape[1] - lanes
    chip = lax.shift_right_logical(me_ref[0], 1)
    first = (me_ref[0] & 1) == 0
    for step in range(chips):
        own = own_ref[step * rows : (step + 1) * rows, :]
        other = other_ref[step * rows : (step + 1) * rows, :]
        source = lax.rem(chip - step + chips, chips)
        pair = jnp.concatenate([jnp.where(first, own, other), jnp.where(first, other, own)], axis=0)
        held_ref[pl.ds(pl.multiple_of(source * 2 * rows, 2 * rows), 2 * rows), :] = pair
    sums_ref[...] = lax.dot_general(
        weight_ref[:, pl.ds(weight_ref.shape[1] - share, share)],
        held_ref[:, pl.ds(0, share)],
        (((1,), (1,)), ((), ())),
        preferred_element_type=jnp.float32,
    )
    lane = lax.broadcasted_iota(jnp.int32, (8, lanes), 1)
    parts = (lane >= scale_lane) & (lane < scale_lane + 3)
    scale = lax.dot_general(
        jnp.where(parts, 1.0, 0.0).astype(jnp.bfloat16),
        held_ref[:, pl.ds(share, lanes)],
        (((1,), (1,)), ((), ())),
        preferred_element_type=jnp.float32,
    )
    scale_ref[...] = scale[0:1]
    riding = jnp.zeros((16, lanes), jnp.float32)
    for source in range(2 * chips):
        riding = riding + held_ref[pl.ds(source * rows, 16), pl.ds(share, lanes)].astype(jnp.float32)
    tokens_of, pairs_of, experts = factors
    usage = (riding[0:1] + riding[1:2] + riding[2:3]) / pairs_of
    shares = (riding[3:4] + riding[4:5] + riding[5:6]) / tokens_of
    product = jnp.where(lane[0:1] < int(experts), usage * shares, 0.0)
    balance_ref[...] = experts * jnp.sum(product, axis=1, keepdims=True)


def ring_project(me, weight_t, own, other, rows, factors):
    columns, width = weight_t.shape
    count, share = 2 * own.shape[0], own.shape[1] - lanes
    vmem = pl.BlockSpec(memory_space=pltpu.VMEM)
    return pl.pallas_call(
        lambda *refs: ring_kernel(rows, factors, *refs),
        in_specs=[pl.BlockSpec(memory_space=pltpu.SMEM), vmem, vmem, vmem],
        out_specs=[vmem, vmem, vmem],
        out_shape=[
            jax.ShapeDtypeStruct((columns, count), jnp.float32),
            jax.ShapeDtypeStruct((1, count), jnp.float32),
            jax.ShapeDtypeStruct((1, 1), jnp.float32),
        ],
        scratch_shapes=[pltpu.VMEM((count, own.shape[1]), jnp.bfloat16)],
        compiler_params=pltpu.CompilerParams(vmem_limit_bytes=24 * MIB),
        cost_estimate=pl.CostEstimate(
            flops=2 * count * share * columns,
            bytes_accessed=2 * (count * share + columns * (width + 2 * count)),
            transcendentals=0,
        ),
        name="ring_project",
    )(me, weight_t, own, other)


def project_kernel(weight_ref, rows_ref, sums_ref, scale_ref, out_ref):
    product = lax.dot_general(
        weight_ref[...],
        rows_ref[...],
        (((1,), (1,)), ((), ())),
        preferred_element_type=jnp.float32,
    )
    out_ref[...] = ((product + sums_ref[...]) * scale_ref[...]).astype(jnp.bfloat16)


def project(weight_t, gathered, sums, scale, steps=2):
    count, share = gathered.shape
    columns = weight_t.shape[0]
    block = count // steps
    return pl.pallas_call(
        project_kernel,
        grid=(steps,),
        in_specs=[
            pl.BlockSpec((columns, share), lambda i: (0, 0)),
            pl.BlockSpec((block, share), lambda i: (i, 0)),
            pl.BlockSpec((columns, block), lambda i: (0, i)),
            pl.BlockSpec((1, block), lambda i: (0, i)),
        ],
        out_specs=pl.BlockSpec((columns, block), lambda i: (0, i)),
        out_shape=jax.ShapeDtypeStruct((columns, count), jnp.bfloat16),
        compiler_params=pltpu.CompilerParams(vmem_limit_bytes=56 * MIB),
        cost_estimate=pl.CostEstimate(
            flops=2 * count * share * columns,
            bytes_accessed=2 * (count * share + columns * (share + 3 * count)),
            transcendentals=0,
        ),
        name="qkv_project",
    )(weight_t, gathered, sums, scale)


def on_device(
    residual, expert_hidden, down_weight, gates, routes, router_probs, norm_gain, qkv_weight
):
    experts = lax.axis_size("tensor")
    rows, width = residual.shape
    slot_count = expert_hidden.shape[1] // experts
    split = width * 3 // 4
    gain = norm_gain.reshape(1, width)
    weight = down_weight[0]

    def slots_of(outputs):
        return lax.all_to_all(
            outputs.reshape(experts, slot_count, -1),
            "tensor",
            split_axis=0,
            concat_axis=0,
            tiled=True,
        ).reshape(experts * slot_count, -1)

    head_slots = slots_of(expert_project(expert_hidden[0], weight, 0, split, 2))
    tail_outputs = expert_project(expert_hidden[0], weight, split, width - split, 1)
    tail_slots = slots_of(tail_outputs)
    pick, sums = pick_matrix(
        routes.T, gates.T, router_probs.T, tail_outputs, slot_count
    )
    depth = 16
    breadth = lax.axis_size("dp") // depth
    lines = [[x * depth + z for z in range(depth)] for x in range(breadth)]
    cross = [[x * depth + z for x in range(breadth)] for z in range(depth)]
    sums = lax.psum(sums, "dp", axis_index_groups=lines)
    head, scaled, sums = combine_first(pick, head_slots, residual, gain, sums)
    gathered = lax.all_gather(scaled, "tensor", axis=0, tiled=True)
    sums = lax.psum(sums, "dp", axis_index_groups=cross)
    fresh, riding = combine_last(pick, tail_slots, head, gain, sums)

    def moved(block, chips):
        pairs = [(i, (i + 2 * chips) % experts) for i in range(experts)]
        return lax.ppermute(block, "tensor", pairs)

    up_1, down_1 = moved(riding, 1), moved(riding, -1)
    up_2, down_2 = moved(riding, 2), moved(riding, -2)
    up_3, down_3 = moved(up_1, 2), moved(down_1, -2)
    up_4 = moved(up_2, 2)
    own = stack([riding, up_1, up_2, up_3, up_4, down_3, down_2, down_1])
    other = lax.ppermute(own, "tensor", [(i, i ^ 1) for i in range(experts)])
    total_tokens = rows * lax.axis_size("dp") * experts
    factors = (float(total_tokens), float(total_tokens * routes.shape[1]), float(experts))
    me = lax.axis_index("tensor").astype(jnp.int32).reshape(1)
    weight_t = qkv_weight.T
    part, scale, balance = ring_project(me, weight_t, own, other, rows, factors)
    projected = project(weight_t, gathered, part, scale).T
    return (fresh, projected, balance.reshape(()))


def solution(mesh):
    in_specs = (
        P(("dp", "tensor"), None),
        P(("dp", "tensor"), None, None),
        P("tensor", None, None),
        P(("dp", "tensor"), None),
        P(("dp", "tensor"), None),
        P(("dp", "tensor"), None),
        P(),
        P(None, "tensor"),
    )
    out_specs = (P(("dp", "tensor"), None), P("dp", "tensor"), P())
    return jax.shard_map(
        on_device, mesh=mesh, in_specs=in_specs, out_specs=out_specs, check_vma=False
    )
```

```python
import jax
import jax.numpy as jnp
from jax import lax
from jax.experimental import pallas as pl
from jax.experimental.pallas import tpu as pltpu
from jax.sharding import PartitionSpec as P

eps = 1e-06
lanes = 128
MIB = 2**20


def expert_kernel(hidden_ref, *refs):
    weight_refs, out_ref = refs[:-1], refs[-1]
    depth = weight_refs[0].shape[0]
    total = None
    for k, weight_ref in enumerate(weight_refs):
        part = jnp.dot(
            hidden_ref[:, k * depth : (k + 1) * depth],
            weight_ref[...],
            preferred_element_type=jnp.float32,
        )
        total = part if total is None else total + part
    out_ref[...] = total.astype(jnp.bfloat16)


def expert_project(hidden, weight, steps=2, parts=1):
    slots, depth = hidden.shape
    width = weight.shape[1]
    block = width // steps
    weight_spec = lambda k: pl.BlockSpec((depth // parts, block), lambda i: (k, i))
    return pl.pallas_call(
        expert_kernel,
        grid=(steps,),
        in_specs=[pl.BlockSpec((slots, depth), lambda i: (0, 0))]
        + [weight_spec(k) for k in range(parts)],
        out_specs=pl.BlockSpec((slots, block), lambda i: (0, i)),
        out_shape=jax.ShapeDtypeStruct((slots, width), jnp.bfloat16),
        compiler_params=pltpu.CompilerParams(vmem_limit_bytes=56 * MIB),
        cost_estimate=pl.CostEstimate(
            flops=2 * slots * depth * width,
            bytes_accessed=2 * (depth * width + slots * (depth + width)),
            transcendentals=0,
        ),
        name="expert_project",
    )(hidden, *([weight] * parts))


def pick_kernel(slot_count, routes_ref, gates_ref, probs_ref, pick_ref, counts_ref, shares_ref):
    top_count, rows = routes_ref.shape
    experts = probs_ref.shape[0]
    count = experts * slot_count
    place = lax.broadcasted_iota(jnp.int32, (count, rows), 0)
    expert = lax.shift_right_logical(place, slot_count.bit_length() - 1)
    slot = (place & (slot_count - 1)).astype(jnp.float32)
    label = lax.broadcasted_iota(jnp.int32, (experts, rows), 0)
    named = jnp.zeros((count, rows), jnp.float32)
    gate = jnp.zeros((count, rows), jnp.float32)
    chosen = jnp.zeros((experts, rows), jnp.float32)
    for j in range(top_count):
        route = routes_ref[j : j + 1, :]
        hit = expert == route
        named = named + jnp.where(hit, 1.0, 0.0)
        gate = gate + jnp.where(hit, gates_ref[j : j + 1, :], 0.0)
        chosen = chosen + jnp.where(label == route, 1.0, 0.0)
    row = lax.broadcasted_iota(jnp.int32, (rows, rows), 0)
    column = lax.broadcasted_iota(jnp.int32, (rows, rows), 1)
    earlier = jnp.where(row < column, 1.0, 0.0).astype(jnp.bfloat16)
    rank = jnp.dot(named.astype(jnp.bfloat16), earlier, preferred_element_type=jnp.float32)
    pick = jnp.where(rank == slot, gate, 0.0)
    high = pick.astype(jnp.bfloat16)
    low = (pick - high.astype(jnp.float32)).astype(jnp.bfloat16)
    pick_ref[...] = jnp.concatenate([high, low], axis=1)
    for sums_ref, values in ((counts_ref, chosen), (shares_ref, probs_ref[...])):
        sums = lax.dot_general(
            jnp.ones((8, rows), jnp.float32),
            values,
            (((1,), (1,)), ((), ())),
            precision=lax.Precision.HIGHEST,
            preferred_element_type=jnp.float32,
        )
        sums_ref[...] = sums[0:1]


def pick_matrix(routes, gates, probs, slot_count):
    experts, rows = probs.shape
    sums = jax.ShapeDtypeStruct((1, experts), jnp.float32)
    return pl.pallas_call(
        lambda *refs: pick_kernel(slot_count, *refs),
        out_shape=[
            jax.ShapeDtypeStruct((experts * slot_count, 2 * rows), jnp.bfloat16),
            sums,
            sums,
        ],
        compiler_params=pltpu.CompilerParams(vmem_limit_bytes=8 * MIB),
        name="pick_matrix",
    )(routes, gates, probs)


def combine_kernel(
    pick_ref,
    slots_ref,
    residual_ref,
    gain_ref,
    counts_ref,
    shares_ref,
    fresh_ref,
    normed_ref,
    ring_ref,
):
    rows, width = residual_ref.shape
    split = normed_ref.shape[1]
    block = 256
    total = jnp.zeros((rows, lanes), jnp.float32)
    pick = pick_ref[...]
    for start in range(0, width, block):
        at = pl.ds(start, block)
        both = lax.dot_general(
            pick,
            slots_ref[:, at],
            (((0,), (0,)), ((), ())),
            preferred_element_type=jnp.float32,
        )
        mixture = both[:rows] + both[rows:]
        fresh = (residual_ref[:, at].astype(jnp.float32) + mixture).astype(jnp.bfloat16)
        fresh_ref[:, at] = fresh
        values = fresh.astype(jnp.float32)
        square = values * values
        for lane in range(0, block, lanes):
            total = total + square[:, lane : lane + lanes]
    mean = jnp.sum(total, axis=1, keepdims=True) / width
    scale = lax.rsqrt(mean + eps)
    for start in range(0, width, block):
        at = pl.ds(start, block)
        values = fresh_ref[:, at].astype(jnp.float32)
        normed = (values * scale * gain_ref[:, at]).astype(jnp.bfloat16)
        if start < split:
            normed_ref[:, at] = normed
        else:
            ring_ref[:, pl.ds(start - split, block)] = normed
    row = lax.broadcasted_iota(jnp.int32, (rows, lanes), 0)
    riding = jnp.zeros((rows, lanes), jnp.float32)
    pad = jnp.zeros((1, lanes - counts_ref.shape[1]), jnp.float32)
    for base, ref in ((0, counts_ref), (3, shares_ref)):
        rest = jnp.concatenate([ref[...], pad], axis=1)
        for part in range(3):
            piece = rest.astype(jnp.bfloat16).astype(jnp.float32)
            rest = rest - piece
            riding = jnp.where(row == base + part, piece, riding)
    ring_ref[:, pl.ds(width - split, lanes)] = riding.astype(jnp.bfloat16)


def combine(pick, slots, residual, gain, counts, shares, split):
    rows, width = residual.shape
    return pl.pallas_call(
        combine_kernel,
        out_shape=[
            jax.ShapeDtypeStruct((rows, width), jnp.bfloat16),
            jax.ShapeDtypeStruct((rows, split), jnp.bfloat16),
            jax.ShapeDtypeStruct((rows, width - split + lanes), jnp.bfloat16),
        ],
        compiler_params=pltpu.CompilerParams(vmem_limit_bytes=16 * MIB),
        cost_estimate=pl.CostEstimate(
            flops=4 * rows * slots.shape[0] * width,
            bytes_accessed=2 * (slots.size + 3 * residual.size),
            transcendentals=0,
        ),
        name="combine_and_norm",
    )(pick, slots, residual, gain, counts, shares)


def stack_kernel(*refs):
    out_ref = refs[-1]
    rows = refs[0].shape[0]
    for place, ref in enumerate(refs[:-1]):
        out_ref[pl.ds(place * rows, rows), :] = ref[...]


def stack(blocks):
    rows, columns = blocks[0].shape
    return pl.pallas_call(
        stack_kernel,
        out_shape=jax.ShapeDtypeStruct((len(blocks) * rows, columns), jnp.bfloat16),
        compiler_params=pltpu.CompilerParams(vmem_limit_bytes=16 * MIB),
        name="stack_blocks",
    )(*blocks)


def ring_kernel(
    rows, factors, me_ref, weight_ref, own_ref, other_ref, sums_ref, balance_ref, held_ref
):
    chips = own_ref.shape[0] // rows
    share = own_ref.shape[1] - lanes
    chip = lax.shift_right_logical(me_ref[0], 1)
    first = (me_ref[0] & 1) == 0
    for step in range(chips):
        own = own_ref[step * rows : (step + 1) * rows, :]
        other = other_ref[step * rows : (step + 1) * rows, :]
        source = lax.rem(chip - step + chips, chips)
        pair = jnp.concatenate([jnp.where(first, own, other), jnp.where(first, other, own)], axis=0)
        held_ref[pl.ds(pl.multiple_of(source * 2 * rows, 2 * rows), 2 * rows), :] = pair
    sums_ref[...] = lax.dot_general(
        weight_ref[:, pl.ds(weight_ref.shape[1] - share, share)],
        held_ref[:, pl.ds(0, share)],
        (((1,), (1,)), ((), ())),
        preferred_element_type=jnp.float32,
    )
    riding = jnp.zeros((16, lanes), jnp.float32)
    for source in range(2 * chips):
        riding = riding + held_ref[pl.ds(source * rows, 16), pl.ds(share, lanes)].astype(jnp.float32)
    tokens_of, pairs_of, experts = factors
    usage = (riding[0:1] + riding[1:2] + riding[2:3]) / pairs_of
    shares = (riding[3:4] + riding[4:5] + riding[5:6]) / tokens_of
    balance_ref[...] = experts * jnp.sum(usage * shares, axis=1, keepdims=True)


def ring_project(me, weight_t, own, other, rows, factors):
    columns, width = weight_t.shape
    count, share = 2 * own.shape[0], own.shape[1] - lanes
    vmem = pl.BlockSpec(memory_space=pltpu.VMEM)
    return pl.pallas_call(
        lambda *refs: ring_kernel(rows, factors, *refs),
        in_specs=[pl.BlockSpec(memory_space=pltpu.SMEM), vmem, vmem, vmem],
        out_specs=[vmem, vmem],
        out_shape=[
            jax.ShapeDtypeStruct((columns, count), jnp.float32),
            jax.ShapeDtypeStruct((1, 1), jnp.float32),
        ],
        scratch_shapes=[pltpu.VMEM((count, own.shape[1]), jnp.bfloat16)],
        compiler_params=pltpu.CompilerParams(vmem_limit_bytes=24 * MIB),
        cost_estimate=pl.CostEstimate(
            flops=2 * count * share * columns,
            bytes_accessed=2 * (count * share + columns * (width + 2 * count)),
            transcendentals=0,
        ),
        name="ring_project",
    )(me, weight_t, own, other)


def project_kernel(weight_ref, rows_ref, sums_ref, out_ref):
    product = lax.dot_general(
        weight_ref[...],
        rows_ref[...],
        (((1,), (1,)), ((), ())),
        preferred_element_type=jnp.float32,
    )
    out_ref[...] = (product + sums_ref[...]).astype(jnp.bfloat16)


def project(weight_t, gathered, sums, steps=2):
    count, share = gathered.shape
    columns = weight_t.shape[0]
    block = count // steps
    return pl.pallas_call(
        project_kernel,
        grid=(steps,),
        in_specs=[
            pl.BlockSpec((columns, share), lambda i: (0, 0)),
            pl.BlockSpec((block, share), lambda i: (i, 0)),
            pl.BlockSpec((columns, block), lambda i: (0, i)),
        ],
        out_specs=pl.BlockSpec((columns, block), lambda i: (0, i)),
        out_shape=jax.ShapeDtypeStruct((columns, count), jnp.bfloat16),
        compiler_params=pltpu.CompilerParams(vmem_limit_bytes=56 * MIB),
        cost_estimate=pl.CostEstimate(
            flops=2 * count * share * columns,
            bytes_accessed=2 * (count * share + columns * (share + 3 * count)),
            transcendentals=0,
        ),
        name="qkv_project",
    )(weight_t, gathered, sums)


def on_device(
    residual, expert_hidden, down_weight, gates, routes, router_probs, norm_gain, qkv_weight
):
    experts = lax.axis_size("tensor")
    rows, width = residual.shape
    slot_count = expert_hidden.shape[1] // experts
    split = width * 5 // 8
    expert_out = expert_project(expert_hidden[0], down_weight[0])
    returned = lax.all_to_all(
        expert_out.reshape(experts, slot_count, width),
        "tensor",
        split_axis=0,
        concat_axis=0,
        tiled=True,
    ).reshape(experts * slot_count, width)
    pick, counts, shares = pick_matrix(routes.T, gates.T, router_probs.T, slot_count)
    depth = 16
    breadth = lax.axis_size("dp") // depth
    lines = [[x * depth + z for z in range(depth)] for x in range(breadth)]
    cross = [[x * depth + z for x in range(breadth)] for z in range(depth)]
    sums = lax.psum((counts, shares), "dp", axis_index_groups=cross)
    sums = lax.psum(sums, "dp", axis_index_groups=lines)
    fresh, normed, riding = combine(
        pick, returned, residual, norm_gain.reshape(1, width), *sums, split
    )
    gathered = lax.all_gather(normed, "tensor", axis=0, tiled=True)
    chips = experts // 2
    up = [(i, (i + 2) % experts) for i in range(experts)]
    down = [(i, (i - 2) % experts) for i in range(experts)]
    ups, downs = [riding], [riding]
    for step in range(chips // 2):
        ups.append(lax.ppermute(ups[-1], "tensor", up))
        if step < chips // 2 - 1:
            downs.append(lax.ppermute(downs[-1], "tensor", down))
    own = stack(ups + downs[:0:-1])
    other = lax.ppermute(own, "tensor", [(i, i ^ 1) for i in range(experts)])
    total_tokens = rows * lax.axis_size("dp") * experts
    factors = (float(total_tokens), float(total_tokens * routes.shape[1]), float(experts))
    me = lax.axis_index("tensor").astype(jnp.int32).reshape(1)
    weight_t = qkv_weight.T
    part, balance = ring_project(me, weight_t, own, other, rows, factors)
    projected = project(weight_t, gathered, part).T
    return (fresh, projected, balance.reshape(()))


def solution(mesh):
    in_specs = (
        P(("dp", "tensor"), None),
        P(("dp", "tensor"), None, None),
        P("tensor", None, None),
        P(("dp", "tensor"), None),
        P(("dp", "tensor"), None),
        P(("dp", "tensor"), None),
        P(),
        P(None, "tensor"),
    )
    out_specs = (P(("dp", "tensor"), None), P("dp", "tensor"), P())
    return jax.shard_map(
        on_device, mesh=mesh, in_specs=in_specs, out_specs=out_specs, check_vma=False
    )
```

```python
import jax
import jax.numpy as jnp
from jax import lax
from jax.experimental import pallas as pl
from jax.experimental.pallas import tpu as pltpu
from jax.sharding import PartitionSpec as P

eps = 1e-06
lanes = 128
MIB = 2**20


def expert_kernel(hidden_ref, *refs):
    weight_refs, out_ref = refs[:-1], refs[-1]
    depth = weight_refs[0].shape[0]
    total = None
    for k, weight_ref in enumerate(weight_refs):
        part = jnp.dot(
            hidden_ref[:, k * depth : (k + 1) * depth],
            weight_ref[...],
            preferred_element_type=jnp.float32,
        )
        total = part if total is None else total + part
    out_ref[...] = total.astype(jnp.bfloat16)


def expert_project(hidden, weight, steps=2, parts=1):
    slots, depth = hidden.shape
    width = weight.shape[1]
    block = width // steps
    weight_spec = lambda k: pl.BlockSpec((depth // parts, block), lambda i: (k, i))
    return pl.pallas_call(
        expert_kernel,
        grid=(steps,),
        in_specs=[pl.BlockSpec((slots, depth), lambda i: (0, 0))]
        + [weight_spec(k) for k in range(parts)],
        out_specs=pl.BlockSpec((slots, block), lambda i: (0, i)),
        out_shape=jax.ShapeDtypeStruct((slots, width), jnp.bfloat16),
        compiler_params=pltpu.CompilerParams(vmem_limit_bytes=56 * MIB),
        cost_estimate=pl.CostEstimate(
            flops=2 * slots * depth * width,
            bytes_accessed=2 * (depth * width + slots * (depth + width)),
            transcendentals=0,
        ),
        name="expert_project",
    )(hidden, *([weight] * parts))


def pick_kernel(slot_count, routes_ref, gates_ref, probs_ref, pick_ref, counts_ref, shares_ref):
    top_count, rows = routes_ref.shape
    experts = probs_ref.shape[0]
    count = experts * slot_count
    place = lax.broadcasted_iota(jnp.int32, (count, rows), 0)
    expert = lax.shift_right_logical(place, slot_count.bit_length() - 1)
    slot = (place & (slot_count - 1)).astype(jnp.float32)
    label = lax.broadcasted_iota(jnp.int32, (experts, rows), 0)
    named = jnp.zeros((count, rows), jnp.float32)
    gate = jnp.zeros((count, rows), jnp.float32)
    chosen = jnp.zeros((experts, rows), jnp.float32)
    for j in range(top_count):
        route = routes_ref[j : j + 1, :]
        hit = expert == route
        named = named + jnp.where(hit, 1.0, 0.0)
        gate = gate + jnp.where(hit, gates_ref[j : j + 1, :], 0.0)
        chosen = chosen + jnp.where(label == route, 1.0, 0.0)
    row = lax.broadcasted_iota(jnp.int32, (rows, rows), 0)
    column = lax.broadcasted_iota(jnp.int32, (rows, rows), 1)
    earlier = jnp.where(row < column, 1.0, 0.0).astype(jnp.bfloat16)
    rank = jnp.dot(named.astype(jnp.bfloat16), earlier, preferred_element_type=jnp.float32)
    pick = jnp.where(rank == slot, gate, 0.0)
    high = pick.astype(jnp.bfloat16)
    low = (pick - high.astype(jnp.float32)).astype(jnp.bfloat16)
    pick_ref[...] = jnp.concatenate([high, low], axis=1)
    for sums_ref, values in ((counts_ref, chosen), (shares_ref, probs_ref[...])):
        sums = lax.dot_general(
            jnp.ones((8, rows), jnp.float32),
            values,
            (((1,), (1,)), ((), ())),
            precision=lax.Precision.HIGHEST,
            preferred_element_type=jnp.float32,
        )
        sums_ref[...] = sums[0:1]


def pick_matrix(routes, gates, probs, slot_count):
    experts, rows = probs.shape
    sums = jax.ShapeDtypeStruct((1, experts), jnp.float32)
    return pl.pallas_call(
        lambda *refs: pick_kernel(slot_count, *refs),
        out_shape=[
            jax.ShapeDtypeStruct((experts * slot_count, 2 * rows), jnp.bfloat16),
            sums,
            sums,
        ],
        compiler_params=pltpu.CompilerParams(vmem_limit_bytes=8 * MIB),
        name="pick_matrix",
    )(routes, gates, probs)


def combine_kernel(
    pick_ref,
    slots_ref,
    residual_ref,
    gain_ref,
    counts_ref,
    shares_ref,
    fresh_ref,
    normed_ref,
    ring_ref,
):
    rows, width = residual_ref.shape
    split = normed_ref.shape[1]
    block = 256
    total = jnp.zeros((rows, lanes), jnp.float32)
    pick = pick_ref[...]
    for start in range(0, width, block):
        at = pl.ds(start, block)
        both = lax.dot_general(
            pick,
            slots_ref[:, at],
            (((0,), (0,)), ((), ())),
            preferred_element_type=jnp.float32,
        )
        mixture = both[:rows] + both[rows:]
        fresh = (residual_ref[:, at].astype(jnp.float32) + mixture).astype(jnp.bfloat16)
        fresh_ref[:, at] = fresh
        values = fresh.astype(jnp.float32)
        square = values * values
        for lane in range(0, block, lanes):
            total = total + square[:, lane : lane + lanes]
    mean = jnp.sum(total, axis=1, keepdims=True) / width
    scale = lax.rsqrt(mean + eps)
    for start in range(0, width, block):
        at = pl.ds(start, block)
        values = fresh_ref[:, at].astype(jnp.float32)
        normed = (values * scale * gain_ref[:, at]).astype(jnp.bfloat16)
        if start < split:
            normed_ref[:, at] = normed
        else:
            ring_ref[:, pl.ds(start - split, block)] = normed
    row = lax.broadcasted_iota(jnp.int32, (rows, lanes), 0)
    riding = jnp.zeros((rows, lanes), jnp.float32)
    pad = jnp.zeros((1, lanes - counts_ref.shape[1]), jnp.float32)
    for base, ref in ((0, counts_ref), (3, shares_ref)):
        rest = jnp.concatenate([ref[...], pad], axis=1)
        for part in range(3):
            piece = rest.astype(jnp.bfloat16).astype(jnp.float32)
            rest = rest - piece
            riding = jnp.where(row == base + part, piece, riding)
    ring_ref[:, pl.ds(width - split, lanes)] = riding.astype(jnp.bfloat16)


def combine(pick, slots, residual, gain, counts, shares, split):
    rows, width = residual.shape
    return pl.pallas_call(
        combine_kernel,
        out_shape=[
            jax.ShapeDtypeStruct((rows, width), jnp.bfloat16),
            jax.ShapeDtypeStruct((rows, split), jnp.bfloat16),
            jax.ShapeDtypeStruct((rows, width - split + lanes), jnp.bfloat16),
        ],
        compiler_params=pltpu.CompilerParams(vmem_limit_bytes=16 * MIB),
        cost_estimate=pl.CostEstimate(
            flops=4 * rows * slots.shape[0] * width,
            bytes_accessed=2 * (slots.size + 3 * residual.size),
            transcendentals=0,
        ),
        name="combine_and_norm",
    )(pick, slots, residual, gain, counts, shares)


def stack_kernel(*refs):
    out_ref = refs[-1]
    rows = refs[0].shape[0]
    for place, ref in enumerate(refs[:-1]):
        out_ref[pl.ds(place * rows, rows), :] = ref[...]


def stack(blocks):
    rows, columns = blocks[0].shape
    return pl.pallas_call(
        stack_kernel,
        out_shape=jax.ShapeDtypeStruct((len(blocks) * rows, columns), jnp.bfloat16),
        compiler_params=pltpu.CompilerParams(vmem_limit_bytes=16 * MIB),
        name="stack_blocks",
    )(*blocks)


def ring_kernel(
    rows, factors, me_ref, weight_ref, own_ref, other_ref, sums_ref, balance_ref, held_ref
):
    chips = own_ref.shape[0] // rows
    share = own_ref.shape[1] - lanes
    chip = lax.shift_right_logical(me_ref[0], 1)
    first = (me_ref[0] & 1) == 0
    for step in range(chips):
        own = own_ref[step * rows : (step + 1) * rows, :]
        other = other_ref[step * rows : (step + 1) * rows, :]
        source = lax.rem(chip - step + chips, chips)
        pair = jnp.concatenate([jnp.where(first, own, other), jnp.where(first, other, own)], axis=0)
        held_ref[pl.ds(pl.multiple_of(source * 2 * rows, 2 * rows), 2 * rows), :] = pair
    sums_ref[...] = lax.dot_general(
        weight_ref[:, pl.ds(weight_ref.shape[1] - share, share)],
        held_ref[:, pl.ds(0, share)],
        (((1,), (1,)), ((), ())),
        preferred_element_type=jnp.float32,
    )
    riding = jnp.zeros((16, lanes), jnp.float32)
    for source in range(2 * chips):
        riding = riding + held_ref[pl.ds(source * rows, 16), pl.ds(share, lanes)].astype(jnp.float32)
    tokens_of, pairs_of, experts = factors
    usage = (riding[0:1] + riding[1:2] + riding[2:3]) / pairs_of
    shares = (riding[3:4] + riding[4:5] + riding[5:6]) / tokens_of
    balance_ref[...] = experts * jnp.sum(usage * shares, axis=1, keepdims=True)


def ring_project(me, weight_t, own, other, rows, factors):
    columns, width = weight_t.shape
    count, share = 2 * own.shape[0], own.shape[1] - lanes
    vmem = pl.BlockSpec(memory_space=pltpu.VMEM)
    return pl.pallas_call(
        lambda *refs: ring_kernel(rows, factors, *refs),
        in_specs=[pl.BlockSpec(memory_space=pltpu.SMEM), vmem, vmem, vmem],
        out_specs=[vmem, vmem],
        out_shape=[
            jax.ShapeDtypeStruct((columns, count), jnp.float32),
            jax.ShapeDtypeStruct((1, 1), jnp.float32),
        ],
        scratch_shapes=[pltpu.VMEM((count, own.shape[1]), jnp.bfloat16)],
        compiler_params=pltpu.CompilerParams(vmem_limit_bytes=24 * MIB),
        cost_estimate=pl.CostEstimate(
            flops=2 * count * share * columns,
            bytes_accessed=2 * (count * share + columns * (width + 2 * count)),
            transcendentals=0,
        ),
        name="ring_project",
    )(me, weight_t, own, other)


def project_kernel(weight_ref, rows_ref, sums_ref, out_ref):
    product = lax.dot_general(
        weight_ref[...],
        rows_ref[...],
        (((1,), (1,)), ((), ())),
        preferred_element_type=jnp.float32,
    )
    out_ref[...] = (product + sums_ref[...]).astype(jnp.bfloat16)


def project(weight_t, gathered, sums, steps=2):
    count, share = gathered.shape
    columns = weight_t.shape[0]
    block = count // steps
    return pl.pallas_call(
        project_kernel,
        grid=(steps,),
        in_specs=[
            pl.BlockSpec((columns, share), lambda i: (0, 0)),
            pl.BlockSpec((block, share), lambda i: (i, 0)),
            pl.BlockSpec((columns, block), lambda i: (0, i)),
        ],
        out_specs=pl.BlockSpec((columns, block), lambda i: (0, i)),
        out_shape=jax.ShapeDtypeStruct((columns, count), jnp.bfloat16),
        compiler_params=pltpu.CompilerParams(vmem_limit_bytes=56 * MIB),
        cost_estimate=pl.CostEstimate(
            flops=2 * count * share * columns,
            bytes_accessed=2 * (count * share + columns * (share + 3 * count)),
            transcendentals=0,
        ),
        name="qkv_project",
    )(weight_t, gathered, sums)


def on_device(
    residual, expert_hidden, down_weight, gates, routes, router_probs, norm_gain, qkv_weight
):
    experts = lax.axis_size("tensor")
    rows, width = residual.shape
    slot_count = expert_hidden.shape[1] // experts
    split = width * 3 // 4
    expert_out = expert_project(expert_hidden[0], down_weight[0])
    returned = lax.all_to_all(
        expert_out.reshape(experts, slot_count, width),
        "tensor",
        split_axis=0,
        concat_axis=0,
        tiled=True,
    ).reshape(experts * slot_count, width)
    pick, counts, shares = pick_matrix(routes.T, gates.T, router_probs.T, slot_count)
    depth = 16
    breadth = lax.axis_size("dp") // depth
    lines = [[x * depth + z for z in range(depth)] for x in range(breadth)]
    cross = [[x * depth + z for x in range(breadth)] for z in range(depth)]
    sums = lax.psum((counts, shares), "dp", axis_index_groups=cross)
    sums = lax.psum(sums, "dp", axis_index_groups=lines)
    fresh, normed, riding = combine(
        pick, returned, residual, norm_gain.reshape(1, width), *sums, split
    )
    gathered = lax.all_gather(normed, "tensor", axis=0, tiled=True)
    chips = experts // 2
    up = [(i, (i + 2) % experts) for i in range(experts)]
    down = [(i, (i - 2) % experts) for i in range(experts)]
    ups, downs = [riding], [riding]
    for step in range(chips // 2):
        ups.append(lax.ppermute(ups[-1], "tensor", up))
        if step < chips // 2 - 1:
            downs.append(lax.ppermute(downs[-1], "tensor", down))
    own = stack(ups + downs[:0:-1])
    other = lax.ppermute(own, "tensor", [(i, i ^ 1) for i in range(experts)])
    total_tokens = rows * lax.axis_size("dp") * experts
    factors = (float(total_tokens), float(total_tokens * routes.shape[1]), float(experts))
    me = lax.axis_index("tensor").astype(jnp.int32).reshape(1)
    weight_t = qkv_weight.T
    part, balance = ring_project(me, weight_t, own, other, rows, factors)
    projected = project(weight_t, gathered, part).T
    return (fresh, projected, balance.reshape(()))


def solution(mesh):
    in_specs = (
        P(("dp", "tensor"), None),
        P(("dp", "tensor"), None, None),
        P("tensor", None, None),
        P(("dp", "tensor"), None),
        P(("dp", "tensor"), None),
        P(("dp", "tensor"), None),
        P(),
        P(None, "tensor"),
    )
    out_specs = (P(("dp", "tensor"), None), P("dp", "tensor"), P())
    return jax.shard_map(
        on_device, mesh=mesh, in_specs=in_specs, out_specs=out_specs, check_vma=False
    )
```
